32 devices in a mesh: space: 8 (over y, x, core), chan: 4 (over z).
Axes of the slice: x: 2, y: 2, z: 4, core: 2. Of those that a mesh axis runs over, the one named last changes fastest.
Arguments:
- activation: bfloat16 [8, 96, 16, 128], P('space', 'chan'), may hold values from -6 to 6
- weights: bfloat16 [3, 3, 3, 96, 96], replicated, may hold values from -0.125 to 0.125
- cotangent: bfloat16 [8, 96, 16, 128], P('space', 'chan'), may hold values from -6 to 6
Outputs:
- output: bfloat16 [8, 96, 16, 128], P('space', 'chan')
- input_grad: bfloat16 [8, 96, 16, 128], P('space', 'chan')
- weight_grad: float32 [3, 3, 3, 96, 96], P(None, None, None, None, 'chan')
The draws below stay inside these ranges and needn't reach their ends.
All inputs are finite; a program needn't handle non-finite values.
Results may differ from the reference program's by a relative error of at most 0.0095.
Values may be sent and summed in bfloat16 or wider, within the bound.
A program may use at most 64 MiB of HBM per device.

```python
import math
import jax
import jax.numpy as jnp
from jax import lax

C = 96
HEIGHT = 16
WIDTH = 128
DEPTH = 8


def level_of(stream_key, dims, cuts, least, largest):
    level, own = 1.0, jax.random.fold_in(stream_key, 6)
    for position, blocks in cuts:
        steps = jnp.exp(jax.random.uniform(jax.random.fold_in(own, position), (blocks,), jnp.float32, least / len(cuts), largest / len(cuts)))
        level = level * jnp.repeat(steps, dims[position] // blocks).reshape([-1 if axis == position else 1 for axis in range(len(dims))])
    return level


def normal_values(own_key, dims, spread, reach, pieces=(), kind=jnp.bfloat16):
    gain = level_of(own_key, dims, pieces, -0.22, 0.18) if pieces else 1.0
    values = jax.random.normal(own_key, dims, jnp.float32) * spread * gain
    return jnp.minimum(jnp.maximum(values, -reach), reach).astype(kind)


def setup_inputs(seed: int = 0) -> dict:
    seeds = jax.random.split(jax.random.key(seed), 4)
    activation = normal_values(seeds[0], (DEPTH, C, HEIGHT, WIDTH), 1.0, 6.0, ((0, 8), (1, 4)))
    weights = normal_values(seeds[1], (3, 3, 3, C, C), (27 * C) ** -0.5, 0.125)
    cotangent = normal_values(seeds[2], (DEPTH, C, HEIGHT, WIDTH), 1.0, 6.0, ((0, 8), (1, 4)))
    return dict(activation=activation, weights=weights, cotangent=cotangent)


def convolve(volume, kernel):
    return lax.conv_general_dilated(volume[None], kernel, (1, 1, 1), ((1, 1), (1, 1), (1, 1)), dimension_numbers=('NDCHW', 'DHWIO', 'NDCHW'), precision=lax.Precision.HIGHEST)[0]

def reference(activation, weights, cotangent):
    source = activation.astype(jnp.float32)
    kernel = weights.astype(jnp.float32)
    signal = cotangent.astype(jnp.float32)
    result, pullback = jax.vjp(convolve, source, kernel)
    source_grad, kernel_grad = pullback(signal)
    scaled = kernel_grad / math.sqrt(DEPTH * HEIGHT * WIDTH)
    return (result.astype(jnp.bfloat16), source_grad.astype(jnp.bfloat16), scaled)
```

```python
import functools
import math

import jax
import jax.numpy as jnp
from jax import lax
from jax.experimental import pallas as pl
from jax.experimental.pallas import tpu as pltpu
from jax.sharding import PartitionSpec as P

BF, F32 = jnp.bfloat16, jnp.float32
LANE = 128


def kernel(space, chan, blk, pad, channels, height, scale,
           a_ref, g_ref, w_ref, out_ref, back_ref, wg_ref,
           ga, gg, x3, gs, wf, wb, s32, t32, r32, z32,
           halo, psend, precv, own, wsend, wrecv, wcur,
           ga_s, ga_r, gg_s, gg_r, h_s, h_r, p_s, p_r, w_s, w_r):
    e = lax.axis_index("space")
    z = lax.axis_index("chan")
    rows = blk * height
    span = height * LANE
    rounds = space.bit_length() - 1
    up, down = lax.rem(e + 1, space), lax.rem(e + space - 1, space)

    def flip(bit):
        return e + bit * (1 - 2 * lax.rem(e // bit, 2))

    barrier = pltpu.get_barrier_semaphore()
    others = [{"chan": lax.rem(z + k, chan)} for k in range(1, chan)]
    others += [{"space": up}, {"space": down}]
    others += [{"space": flip(1 << r)} for r in range(rounds)]
    for other in others:
        pl.semaphore_signal(barrier, inc=1, device_id=other)
    pl.semaphore_wait(barrier, len(others))

    def gather(src, dst, ssem, rsem):
        return [
            pltpu.make_async_remote_copy(
                src, dst.at[z], ssem.at[k], rsem.at[k],
                device_id={"chan": lax.rem(z + k, chan)})
            for k in range(1, chan)
        ]

    def edge(src, dst, ssem, rsem, to):
        return pltpu.make_async_remote_copy(src, dst, ssem, rsem, device_id={"space": to})

    copies_a = gather(a_ref, ga, ga_s, ga_r)
    copies_g = gather(g_ref, gg, gg_s, gg_r)
    halo_up = edge(g_ref, halo.at[0], h_s.at[0], h_r.at[0], up)
    halo_down = edge(g_ref, halo.at[1], h_s.at[1], h_r.at[1], down)
    has_up, has_down = e < space - 1, e > 0

    for c in copies_a:
        c.start()
    pl.when(has_up)(halo_up.start)
    pl.when(has_down)(halo_down.start)
    for c in copies_g:
        c.start()

    def no_lower():
        halo[0] = jnp.zeros((rows, LANE), BF)
        precv[0] = jnp.zeros((rows, LANE), BF)
        precv[2] = jnp.zeros((rows, LANE), BF)

    def no_upper():
        halo[1] = jnp.zeros((rows, LANE), BF)
        precv[1] = jnp.zeros((rows, LANE), BF)
        precv[3] = jnp.zeros((rows, LANE), BF)

    pl.when(e == 0)(no_lower)
    pl.when(e == space - 1)(no_upper)
    ga[z] = a_ref[...]
    gg[z] = g_ref[...]

    x3[...] = jnp.zeros_like(x3)
    wf[...] = jnp.zeros_like(wf)
    wb[...] = jnp.zeros_like(wb)
    z32[...] = jnp.zeros_like(z32)
    row = lax.broadcasted_iota(jnp.int32, (pad, channels), 0)
    col = lax.broadcasted_iota(jnp.int32, (pad, channels), 1)
    pick = jnp.where((col == row + z * blk) & (row < blk), 1.0, 0.0).astype(BF)
    for a in range(3):
        for b in range(3):
            for c in range(3):
                at = (pl.ds((b * 3 + a) * pad, pad), pl.ds(c * LANE, channels))
                tap = w_ref[(a * 3 + b) * 3 + c]
                wf[at] = lax.dot_general(
                    pick, tap, (((1,), (1,)), ((), ())),
                    preferred_element_type=F32).astype(BF)
                tap = w_ref[26 - ((a * 3 + b) * 3 + c)]
                wb[at] = jnp.dot(pick, tap, preferred_element_type=F32).astype(BF)

    lane = lax.broadcasted_iota(jnp.int32, (channels * height, LANE), 1)

    def spread(src):
        v = src[...].reshape(channels * height, LANE).astype(F32)
        s32[0] = jnp.where(lane == 0, 0.0, pltpu.roll(v, 1, 1))
        s32[1] = v
        s32[2] = jnp.where(lane == LANE - 1, 0.0, pltpu.roll(v, LANE - 1, 1))
        for c in range(3):
            for h in range(height):
                x3[c * LANE:c * LANE + channels, (h + 1) * LANE:(h + 2) * LANE] = (
                    s32[c, pl.ds(h, channels, stride=height), :].astype(BF))

    def conv(w, slot, keep):
        r32[...] = jnp.dot(w[...], x3[:, LANE:LANE + span], preferred_element_type=F32)
        for a in range(3):
            for h in range(height):
                def part(b, hh):
                    return r32[(b * 3 + a) * pad:(b * 3 + a + 1) * pad, hh * LANE:(hh + 1) * LANE]
                v = part(1, h)
                if h > 0:
                    v = v + part(0, h - 1)
                if h < height - 1:
                    v = v + part(2, h + 1)
                t32[a, pl.ds(h, pad, stride=height), :] = v
        psend[slot] = t32[0, 0:rows, :].astype(BF)
        psend[slot + 1] = t32[2, 0:rows, :].astype(BF)
        own[keep] = t32[1, 0:rows, :]

    def partials(slot):
        return (edge(psend.at[slot], precv.at[slot], p_s.at[slot], p_r.at[slot], up),
                edge(psend.at[slot + 1], precv.at[slot + 1], p_s.at[slot + 1],
                     p_r.at[slot + 1], down))

    def finish(pair, slot, keep, ref):
        pl.when(has_down)(pair[0].wait_recv)
        pl.when(has_up)(pair[1].wait_recv)
        ref[...] = (own[keep] + precv[slot].astype(F32)
                    + precv[slot + 1].astype(F32)).astype(BF)

    for c in copies_a:
        c.wait_recv()
    spread(ga)
    conv(wf, 0, 0)
    pair_out = partials(0)
    pl.when(has_up)(pair_out[0].start)
    pl.when(has_down)(pair_out[1].start)

    pl.when(has_down)(halo_up.wait_recv)
    pl.when(has_up)(halo_down.wait_recv)
    for a in range(3):
        src = halo[1] if a == 0 else g_ref[...] if a == 1 else halo[0]
        z32[0:rows, :] = src.astype(F32)
        for h in range(height):
            gs[a * pad:(a + 1) * pad, h * LANE:(h + 1) * LANE] = (
                z32[pl.ds(h, pad, stride=height), :].astype(BF))
    for b in range(3):
        wcur[b] = lax.dot_general(
            gs[...], x3[:, b * LANE:b * LANE + span], (((1,), (1,)), ((), ())),
            preferred_element_type=F32)

    def exchange(r):
        return edge(wsend.at[r], wrecv.at[r], w_s.at[r], w_r.at[r], flip(1 << r))

    swaps = [exchange(r) for r in range(rounds)]

    def begin(r):
        wsend[r] = wcur[...].astype(BF)
        swaps[r].start()

    def end(r):
        swaps[r].wait_recv()
        wcur[...] = wsend[r].astype(F32) + wrecv[r].astype(F32)

    begin(0)
    end(0)
    if rounds > 1:
        begin(1)
    for c in copies_g:
        c.wait_recv()
    spread(gg)
    conv(wb, 2, 1)
    pair_back = partials(2)
    pl.when(has_up)(pair_back[0].start)
    pl.when(has_down)(pair_back[1].start)
    for r in range(1, rounds):
        end(r)
        if r + 1 < rounds:
            begin(r + 1)
        if r == 1:
            finish(pair_out, 0, 0, out_ref)
    if rounds < 2:
        finish(pair_out, 0, 0, out_ref)
    wg_ref[...] = wcur[...] * scale
    finish(pair_back, 2, 1, back_ref)

    for c in copies_a + copies_g + swaps:
        c.wait_send()
    for c in (halo_up, pair_out[0], pair_back[0]):
        pl.when(has_up)(c.wait_send)
    for c in (halo_down, pair_out[1], pair_back[1]):
        pl.when(has_down)(c.wait_send)


def body(space, chan, activation, weights, cotangent):
    planes, blk, height, width = activation.shape
    channels = weights.shape[3]
    assert planes == 1 and width == LANE and space & (space - 1) == 0
    pad = -(-blk // 16) * 16
    rows = blk * height
    rounds = space.bit_length() - 1
    scale = 1.0 / math.sqrt(planes * space * height * width)
    dma = pltpu.SemaphoreType.DMA
    vm = pltpu.VMEM
    wide = (height + 2) * LANE
    out, back, grads = pl.pallas_call(
        functools.partial(kernel, space, chan, blk, pad, channels, height, scale),
        out_shape=(
            jax.ShapeDtypeStruct((rows, LANE), BF),
            jax.ShapeDtypeStruct((rows, LANE), BF),
            jax.ShapeDtypeStruct((3, 3 * pad, 3 * LANE), F32),
        ),
        in_specs=[pl.BlockSpec(memory_space=pltpu.VMEM)] * 3,
        out_specs=[pl.BlockSpec(memory_space=pltpu.VMEM)] * 3,
        scratch_shapes=[
            vm((chan, rows, LANE), BF),
            vm((chan, rows, LANE), BF),
            vm((3 * LANE, wide), BF),
            vm((3 * pad, height * LANE), BF),
            vm((9 * pad, 3 * LANE), BF),
            vm((9 * pad, 3 * LANE), BF),
            vm((3, channels * height, LANE), F32),
            vm((3, pad * height, LANE), F32),
            vm((9 * pad, height * LANE), F32),
            vm((pad * height, LANE), F32),
            vm((2, rows, LANE), BF),
            vm((4, rows, LANE), BF),
            vm((4, rows, LANE), BF),
            vm((2, rows, LANE), F32),
            vm((rounds, 3, 3 * pad, 3 * LANE), BF),
            vm((rounds, 3, 3 * pad, 3 * LANE), BF),
            vm((3, 3 * pad, 3 * LANE), F32),
            dma((chan,)), dma((chan,)), dma((chan,)), dma((chan,)),
            dma((2,)), dma((2,)), dma((4,)), dma((4,)),
            dma((rounds,)), dma((rounds,)),
        ],
        compiler_params=pltpu.CompilerParams(
            collective_id=0, has_side_effects=True, vmem_limit_bytes=40 * 2**20),
    )(activation.reshape(rows, width), cotangent.reshape(rows, width),
      weights.reshape(27, channels, channels))
    field = (1, blk, height, width)
    grads = grads.reshape(3, 3, pad, 3, LANE)[:, :, :blk, :, :channels]
    grads = jnp.transpose(grads, (1, 0, 3, 4, 2))
    return out.reshape(field), back.reshape(field), grads


def solution(mesh):
    field = P("space", "chan", None, None)
    return jax.shard_map(
        functools.partial(body, mesh.shape["space"], mesh.shape["chan"]),
        mesh=mesh,
        in_specs=(field, P(), field),
        out_specs=(field, field, P(None, None, None, None, "chan")),
        check_vma=False,
    )
```

```python
import functools
import math

import jax
import jax.numpy as jnp
from jax import lax
from jax.experimental import pallas as pl
from jax.experimental.pallas import tpu as pltpu
from jax.sharding import PartitionSpec as P

BF, F32 = jnp.bfloat16, jnp.float32
LANE = 128


def kernel(space, chan, blk, pad, channels, height, scale,
           a_ref, g_ref, w_ref, out_ref, back_ref, wg_ref,
           ga, x3, xg, wf, wb, s32, t32, r32, z32, part,
           halo, psend, precv, wflat, wsend, wrecv, wfull,
           rsend, rrecv,
           g_s, g_r, h_s, h_r, p_s, p_r, w_s, w_r, f_s, f_r, r_s, r_r):
    e = lax.axis_index("space")
    z = lax.axis_index("chan")
    rows = blk * height
    span = height * LANE
    up, down = lax.rem(e + 1, space), lax.rem(e + space - 1, space)

    def along_z(k):
        return lax.rem(z + k, chan)

    def along_e(k):
        return lax.rem(e + k, space)

    barrier = pltpu.get_barrier_semaphore()
    others = [{"chan": along_z(k)} for k in range(1, chan)]
    others += [{"space": along_e(k)} for k in range(1, space)]
    for other in others:
        pl.semaphore_signal(barrier, inc=1, device_id=other)
    pl.semaphore_wait(barrier, len(others))

    def send(src, dst, ssem, rsem, to):
        return pltpu.make_async_remote_copy(src, dst, ssem, rsem, device_id=to)

    gathers = [send(a_ref, ga.at[z], g_s.at[k], g_r.at[k], {"chan": along_z(k)})
               for k in range(1, chan)]

    halo_up = send(g_ref, halo.at[0], h_s.at[0], h_r.at[0], {"space": up})
    halo_down = send(g_ref, halo.at[1], h_s.at[1], h_r.at[1], {"space": down})
    has_up, has_down = e < space - 1, e > 0

    for c in gathers:
        c.start()
    pl.when(has_up)(halo_up.start)
    pl.when(has_down)(halo_down.start)

    def no_lower():
        halo[0] = jnp.zeros((rows, LANE), BF)
        precv[0] = jnp.zeros((rows, LANE), BF)

    def no_upper():
        halo[1] = jnp.zeros((rows, LANE), BF)
        precv[1] = jnp.zeros((rows, LANE), BF)

    pl.when(e == 0)(no_lower)
    pl.when(e == space - 1)(no_upper)
    ga[z] = a_ref[...]

    wide = 9 * pad
    first = lax.broadcasted_iota(jnp.int32, (channels, wide), 0) - z * blk
    place = lax.broadcasted_iota(jnp.int32, (channels, wide), 1)
    inside = (first >= 0) & (first < blk)
    for b in range(3):
        total = jnp.zeros((channels, wide), F32)
        for c in range(3):
            for a in range(3):
                spot = inside & (place == first + (c * 3 + a) * pad)
                tap = w_ref[(a * 3 + 2 - b) * 3 + 2 - c]
                total = total + jnp.dot(
                    tap, jnp.where(spot, 1.0, 0.0).astype(BF), preferred_element_type=F32)
        wb[b * channels:(b + 1) * channels, :] = total.astype(BF)

    z32[...] = jnp.zeros_like(z32)
    few = lax.broadcasted_iota(jnp.int32, (rows, LANE), 1)

    def fill(a, src):
        v = src.astype(F32)
        z32[0, 0:rows, :] = jnp.where(few == 0, 0.0, pltpu.roll(v, 1, 1))
        z32[1, 0:rows, :] = v
        z32[2, 0:rows, :] = jnp.where(few == LANE - 1, 0.0, pltpu.roll(v, LANE - 1, 1))
        for c in range(3):
            at = (c * 3 + a) * pad
            for h in range(height):
                xg[at:at + pad, h * LANE:(h + 1) * LANE] = (
                    z32[c, pl.ds(h, pad, stride=height), :].astype(BF))

    fill(1, g_ref[...])
    pl.when(has_down)(halo_up.wait_recv)
    fill(2, halo[0])
    pl.when(has_up)(halo_down.wait_recv)
    fill(0, halo[1])

    def shifted(count, first_row, group, h):
        def piece(b, hh):
            at = first_row + b * group
            return r32[at:at + count, hh * LANE:(hh + 1) * LANE]
        v = piece(1, h)
        if h > 0:
            v = v + piece(0, h - 1)
        if h < height - 1:
            v = v + piece(2, h + 1)
        return v

    r32[0:3 * channels, :] = jnp.dot(wb[...], xg[...], preferred_element_type=F32)
    for h in range(height):
        part[pl.ds(h, channels, stride=height), :] = shifted(channels, 0, channels, h)

    sums = [send(rsend.at[k], rrecv.at[k], r_s.at[k], r_r.at[k], {"chan": along_z(k)})
            for k in range(1, chan)]

    def block(t):
        return part[pl.ds(pl.multiple_of(t * rows, 16), rows), :]

    for k in range(1, chan):
        rsend[k] = block(along_z(k)).astype(BF)
        sums[k - 1].start()

    x3[...] = jnp.zeros_like(x3)
    wf[...] = jnp.zeros_like(wf)
    row = lax.broadcasted_iota(jnp.int32, (pad, channels), 0)
    col = lax.broadcasted_iota(jnp.int32, (pad, channels), 1)
    pick = jnp.where((col == row + z * blk) & (row < blk), 1.0, 0.0).astype(BF)
    for a in range(3):
        for b in range(3):
            for c in range(3):
                wf[pl.ds((b * 3 + a) * pad, pad), pl.ds(c * LANE, channels)] = (
                    lax.dot_general(
                        pick, w_ref[(a * 3 + b) * 3 + c], (((1,), (1,)), ((), ())),
                        preferred_element_type=F32).astype(BF))

    for c in gathers:
        c.wait_recv()
    lane = lax.broadcasted_iota(jnp.int32, (channels * height, LANE), 1)
    v = ga[...].reshape(channels * height, LANE).astype(F32)
    s32[0] = jnp.where(lane == 0, 0.0, pltpu.roll(v, 1, 1))
    s32[1] = v
    s32[2] = jnp.where(lane == LANE - 1, 0.0, pltpu.roll(v, LANE - 1, 1))
    for c in range(3):
        for h in range(height):
            x3[c * LANE:c * LANE + channels, (h + 1) * LANE:(h + 2) * LANE] = (
                s32[c, pl.ds(h, channels, stride=height), :].astype(BF))

    signal = xg[3 * pad:6 * pad, :]
    for b in range(3):
        share = lax.dot_general(
            signal, x3[:, b * LANE:b * LANE + span], (((1,), (1,)), ((), ())),
            preferred_element_type=F32)
        for c in range(3):
            at = (c * 9 + b * 3) * pad
            wflat[at:at + 3 * pad, :] = share[:, c * LANE:(c + 1) * LANE]
    total_rows = wflat.shape[0]
    chunk = total_rows // space
    if total_rows > 27 * pad:
        wflat[27 * pad:total_rows, :] = jnp.zeros((total_rows - 27 * pad, LANE), F32)
    wsend[...] = wflat[...].astype(BF).reshape(space, chunk, LANE)
    shares = [send(wsend.at[along_e(k)], wrecv.at[k], w_s.at[k], w_r.at[k],
                   {"space": along_e(k)}) for k in range(1, space)]
    for c in shares:
        c.start()

    r32[0:9 * pad, :] = jnp.dot(wf[...], x3[:, LANE:LANE + span], preferred_element_type=F32)

    def relay(a):
        for h in range(height):
            t32[a, pl.ds(h, pad, stride=height), :] = shifted(pad, a * pad, 3 * pad, h)

    relay(0)
    psend[0] = t32[0, 0:rows, :].astype(BF)
    pair = (send(psend.at[0], precv.at[0], p_s.at[0], p_r.at[0], {"space": up}),
            send(psend.at[1], precv.at[1], p_s.at[1], p_r.at[1], {"space": down}))
    pl.when(has_up)(pair[0].start)
    relay(2)
    psend[1] = t32[2, 0:rows, :].astype(BF)
    pl.when(has_down)(pair[1].start)

    relay(1)
    for c in shares:
        c.wait_recv()
    mine = wflat[pl.ds(pl.multiple_of(e * chunk, 16), chunk), :]
    for k in range(1, space):
        mine = mine + wrecv[k].astype(F32)
    wfull[e] = mine.astype(BF)
    fulls = [send(wfull.at[e], wfull.at[e], f_s.at[k], f_r.at[k], {"space": along_e(k)})
             for k in range(1, space)]
    for c in fulls:
        c.start()

    pl.when(has_down)(pair[0].wait_recv)
    pl.when(has_up)(pair[1].wait_recv)
    out_ref[...] = (t32[1, 0:rows, :] + precv[0].astype(F32)
                    + precv[1].astype(F32)).astype(BF)

    for c in sums:
        c.wait_recv()
    total = block(z)
    for k in range(1, chan):
        total = total + rrecv[k].astype(F32)
    back_ref[...] = total.astype(BF)

    for c in fulls:
        c.wait_recv()
    wflat[...] = wfull[...].reshape(total_rows, LANE).astype(F32) * scale
    for a in range(3):
        for b in range(3):
            for c in range(3):
                at = (c * 9 + b * 3 + a) * pad
                wg_ref[(a * 3 + b) * 3 + c] = wflat[at:at + blk, 0:channels]

    for c in gathers + sums + shares + fulls:
        c.wait_send()
    for c in (halo_up, pair[0]):
        pl.when(has_up)(c.wait_send)
    for c in (halo_down, pair[1]):
        pl.when(has_down)(c.wait_send)


def body(space, chan, activation, weights, cotangent):
    planes, blk, height, width = activation.shape
    channels = weights.shape[3]
    assert planes == 1 and width == LANE
    pad = -(-blk // 16) * 16
    rows = blk * height
    scale = 1.0 / math.sqrt(planes * space * height * width)
    dma = pltpu.SemaphoreType.DMA
    vm = pltpu.VMEM
    wide = (height + 2) * LANE
    chunk = -(-27 * pad // (16 * space)) * 16
    out, back, grads = pl.pallas_call(
        functools.partial(kernel, space, chan, blk, pad, channels, height, scale),
        out_shape=(
            jax.ShapeDtypeStruct((rows, LANE), BF),
            jax.ShapeDtypeStruct((rows, LANE), BF),
            jax.ShapeDtypeStruct((27, blk, channels), F32),
        ),
        in_specs=[pl.BlockSpec(memory_space=pltpu.VMEM)] * 3,
        out_specs=[pl.BlockSpec(memory_space=pltpu.VMEM)] * 3,
        scratch_shapes=[
            vm((chan, rows, LANE), BF),
            vm((3 * LANE, wide), BF),
            vm((9 * pad, height * LANE), BF),
            vm((9 * pad, 3 * LANE), BF),
            vm((3 * channels, 9 * pad), BF),
            vm((3, channels * height, LANE), F32),
            vm((3, pad * height, LANE), F32),
            vm((max(9 * pad, 3 * channels), height * LANE), F32),
            vm((3, pad * height, LANE), F32),
            vm((channels * height, LANE), F32),
            vm((2, rows, LANE), BF),
            vm((2, rows, LANE), BF),
            vm((2, rows, LANE), BF),
            vm((space * chunk, LANE), F32),
            vm((space, chunk, LANE), BF),
            vm((space, chunk, LANE), BF),
            vm((space, chunk, LANE), BF),
            vm((chan, rows, LANE), BF),
            vm((chan, rows, LANE), BF),
            dma((chan,)), dma((chan,)), dma((2,)), dma((2,)), dma((2,)), dma((2,)),
            dma((space,)), dma((space,)), dma((space,)), dma((space,)),
            dma((chan,)), dma((chan,)),
        ],
        compiler_params=pltpu.CompilerParams(
            collective_id=0, has_side_effects=True, vmem_limit_bytes=40 * 2**20),
    )(activation.reshape(rows, width), cotangent.reshape(rows, width),
      weights.reshape(27, channels, channels))
    field = (1, blk, height, width)
    grads = jnp.swapaxes(grads.reshape(3, 3, 3, blk, channels), 3, 4)
    return out.reshape(field), back.reshape(field), grads


def solution(mesh):
    field = P("space", "chan", None, None)
    return jax.shard_map(
        functools.partial(body, mesh.shape["space"], mesh.shape["chan"]),
        mesh=mesh,
        in_specs=(field, P(), field),
        out_specs=(field, field, P(None, None, None, None, "chan")),
        check_vma=False,
    )
```

```python
import functools
import math

import jax
import jax.numpy as jnp
from jax import lax
from jax.experimental import pallas as pl
from jax.experimental.pallas import tpu as pltpu
from jax.sharding import PartitionSpec as P

BF, F32 = jnp.bfloat16, jnp.float32
LANE = 128


def kernel(space, chan, blk, pad, channels, height, scale,
           a_ref, g_ref, w_ref, out_ref, back_ref, wg_ref,
           ga, x3, xg, wf, wb, s32, t32, r32, z32, part,
           halo, psend, precv, wflat, wsend, wrecv, wfull,
           rsend, rrecv,
           g_s, g_r, h_s, h_r, p_s, p_r, w_s, w_r, f_s, f_r, r_s, r_r):
    e = lax.axis_index("space")
    z = lax.axis_index("chan")
    rows = blk * height
    span = height * LANE
    up, down = lax.rem(e + 1, space), lax.rem(e + space - 1, space)

    def along_z(k):
        return lax.rem(z + k, chan)

    def along_e(k):
        return lax.rem(e + k, space)

    barrier = pltpu.get_barrier_semaphore()
    others = [{"chan": along_z(k)} for k in range(1, chan)]
    others += [{"space": along_e(k)} for k in range(1, space)]
    for other in others:
        pl.semaphore_signal(barrier, inc=1, device_id=other)
    pl.semaphore_wait(barrier, len(others))

    def send(src, dst, ssem, rsem, to):
        return pltpu.make_async_remote_copy(src, dst, ssem, rsem, device_id=to)

    gathers = [send(a_ref, ga.at[z], g_s.at[k], g_r.at[k], {"chan": along_z(k)})
               for k in range(1, chan)]

    halo_up = send(g_ref, halo.at[0], h_s.at[0], h_r.at[0], {"space": up})
    halo_down = send(g_ref, halo.at[1], h_s.at[1], h_r.at[1], {"space": down})
    has_up, has_down = e < space - 1, e > 0

    for c in gathers:
        c.start()
    pl.when(has_up)(halo_up.start)
    pl.when(has_down)(halo_down.start)

    def no_lower():
        halo[0] = jnp.zeros((rows, LANE), BF)
        precv[0] = jnp.zeros((rows, LANE), BF)

    def no_upper():
        halo[1] = jnp.zeros((rows, LANE), BF)
        precv[1] = jnp.zeros((rows, LANE), BF)

    pl.when(e == 0)(no_lower)
    pl.when(e == space - 1)(no_upper)
    ga[z] = a_ref[...]

    wide = 9 * pad
    first = lax.broadcasted_iota(jnp.int32, (channels, wide), 0) - z * blk
    place = lax.broadcasted_iota(jnp.int32, (channels, wide), 1)
    inside = (first >= 0) & (first < blk)
    for b in range(3):
        total = jnp.zeros((channels, wide), F32)
        for c in range(3):
            for a in range(3):
                spot = inside & (place == first + (c * 3 + a) * pad)
                tap = w_ref[(a * 3 + 2 - b) * 3 + 2 - c]
                total = total + jnp.dot(
                    tap, jnp.where(spot, 1.0, 0.0).astype(BF), preferred_element_type=F32)
        wb[b * channels:(b + 1) * channels, :] = total.astype(BF)

    z32[...] = jnp.zeros_like(z32)
    few = lax.broadcasted_iota(jnp.int32, (rows, LANE), 1)

    def fill(a, src):
        v = src.astype(F32)
        z32[0, 0:rows, :] = jnp.where(few == 0, 0.0, pltpu.roll(v, 1, 1))
        z32[1, 0:rows, :] = v
        z32[2, 0:rows, :] = jnp.where(few == LANE - 1, 0.0, pltpu.roll(v, LANE - 1, 1))
        for c in range(3):
            at = (c * 3 + a) * pad
            for h in range(height):
                xg[at:at + pad, h * LANE:(h + 1) * LANE] = (
                    z32[c, pl.ds(h, pad, stride=height), :].astype(BF))

    fill(1, g_ref[...])
    pl.when(has_down)(halo_up.wait_recv)
    fill(2, halo[0])
    pl.when(has_up)(halo_down.wait_recv)
    fill(0, halo[1])

    def shifted(count, first_row, group, h):
        def piece(b, hh):
            at = first_row + b * group
            return r32[at:at + count, hh * LANE:(hh + 1) * LANE]
        v = piece(1, h)
        if h > 0:
            v = v + piece(0, h - 1)
        if h < height - 1:
            v = v + piece(2, h + 1)
        return v

    r32[0:3 * channels, :] = jnp.dot(wb[...], xg[...], preferred_element_type=F32)
    for h in range(height):
        part[pl.ds(h, channels, stride=height), :] = shifted(channels, 0, channels, h)

    sums = [send(rsend.at[k], rrecv.at[k], r_s.at[k], r_r.at[k], {"chan": along_z(k)})
            for k in range(1, chan)]

    def block(t):
        return part[pl.ds(pl.multiple_of(t * rows, 16), rows), :]

    for k in range(1, chan):
        rsend[k] = block(along_z(k)).astype(BF)

    x3[...] = jnp.zeros_like(x3)
    wf[...] = jnp.zeros_like(wf)
    row = lax.broadcasted_iota(jnp.int32, (pad, channels), 0)
    col = lax.broadcasted_iota(jnp.int32, (pad, channels), 1)
    pick = jnp.where((col == row + z * blk) & (row < blk), 1.0, 0.0).astype(BF)
    for a in range(3):
        for b in range(3):
            for c in range(3):
                wf[pl.ds((b * 3 + a) * pad, pad), pl.ds(c * LANE, channels)] = (
                    lax.dot_general(
                        pick, w_ref[(a * 3 + b) * 3 + c], (((1,), (1,)), ((), ())),
                        preferred_element_type=F32).astype(BF))

    for c in gathers:
        c.wait_recv()
    for c in sums:
        c.start()
    lane = lax.broadcasted_iota(jnp.int32, (channels * height, LANE), 1)
    v = ga[...].reshape(channels * height, LANE).astype(F32)
    s32[0] = jnp.where(lane == 0, 0.0, pltpu.roll(v, 1, 1))
    s32[1] = v
    s32[2] = jnp.where(lane == LANE - 1, 0.0, pltpu.roll(v, LANE - 1, 1))
    for c in range(3):
        for h in range(height):
            x3[c * LANE:c * LANE + channels, (h + 1) * LANE:(h + 2) * LANE] = (
                s32[c, pl.ds(h, channels, stride=height), :].astype(BF))

    signal = xg[3 * pad:6 * pad, :]
    for b in range(3):
        share = lax.dot_general(
            signal, x3[:, b * LANE:b * LANE + span], (((1,), (1,)), ((), ())),
            preferred_element_type=F32)
        for c in range(3):
            at = (c * 9 + b * 3) * pad
            wflat[at:at + 3 * pad, :] = share[:, c * LANE:(c + 1) * LANE]
    total_rows = wflat.shape[0]
    chunk = total_rows // space
    if total_rows > 27 * pad:
        wflat[27 * pad:total_rows, :] = jnp.zeros((total_rows - 27 * pad, LANE), F32)
    wsend[...] = wflat[...].astype(BF).reshape(space, chunk, LANE)
    shares = [send(wsend.at[along_e(k)], wrecv.at[k], w_s.at[k], w_r.at[k],
                   {"space": along_e(k)}) for k in range(1, space)]
    for c in shares:
        c.start()

    r32[0:9 * pad, :] = jnp.dot(wf[...], x3[:, LANE:LANE + span], preferred_element_type=F32)

    def relay(a):
        for h in range(height):
            t32[a, pl.ds(h, pad, stride=height), :] = shifted(pad, a * pad, 3 * pad, h)

    relay(0)
    psend[0] = t32[0, 0:rows, :].astype(BF)
    pair = (send(psend.at[0], precv.at[0], p_s.at[0], p_r.at[0], {"space": up}),
            send(psend.at[1], precv.at[1], p_s.at[1], p_r.at[1], {"space": down}))
    pl.when(has_up)(pair[0].start)
    relay(2)
    psend[1] = t32[2, 0:rows, :].astype(BF)
    pl.when(has_down)(pair[1].start)

    relay(1)
    for c in shares:
        c.wait_recv()
    mine = wflat[pl.ds(pl.multiple_of(e * chunk, 16), chunk), :]
    for k in range(1, space):
        mine = mine + wrecv[k].astype(F32)
    wfull[e] = mine.astype(BF)
    fulls = [send(wfull.at[e], wfull.at[e], f_s.at[k], f_r.at[k], {"space": along_e(k)})
             for k in range(1, space)]
    for c in fulls:
        c.start()

    pl.when(has_down)(pair[0].wait_recv)
    pl.when(has_up)(pair[1].wait_recv)
    out_ref[...] = (t32[1, 0:rows, :] + precv[0].astype(F32)
                    + precv[1].astype(F32)).astype(BF)

    for c in sums:
        c.wait_recv()
    total = block(z)
    for k in range(1, chan):
        total = total + rrecv[k].astype(F32)
    back_ref[...] = total.astype(BF)

    for c in fulls:
        c.wait_recv()
    wflat[...] = wfull[...].reshape(total_rows, LANE).astype(F32) * scale
    for a in range(3):
        for b in range(3):
            for c in range(3):
                at = (c * 9 + b * 3 + a) * pad
                wg_ref[(a * 3 + b) * 3 + c] = wflat[at:at + blk, 0:channels]

    for c in gathers + sums + shares + fulls:
        c.wait_send()
    for c in (halo_up, pair[0]):
        pl.when(has_up)(c.wait_send)
    for c in (halo_down, pair[1]):
        pl.when(has_down)(c.wait_send)


def body(space, chan, activation, weights, cotangent):
    planes, blk, height, width = activation.shape
    channels = weights.shape[3]
    assert planes == 1 and width == LANE
    pad = -(-blk // 16) * 16
    rows = blk * height
    scale = 1.0 / math.sqrt(planes * space * height * width)
    dma = pltpu.SemaphoreType.DMA
    vm = pltpu.VMEM
    wide = (height + 2) * LANE
    chunk = -(-27 * pad // (16 * space)) * 16
    out, back, grads = pl.pallas_call(
        functools.partial(kernel, space, chan, blk, pad, channels, height, scale),
        out_shape=(
            jax.ShapeDtypeStruct((rows, LANE), BF),
            jax.ShapeDtypeStruct((rows, LANE), BF),
            jax.ShapeDtypeStruct((27, blk, channels), F32),
        ),
        in_specs=[pl.BlockSpec(memory_space=pltpu.VMEM)] * 3,
        out_specs=[pl.BlockSpec(memory_space=pltpu.VMEM)] * 3,
        scratch_shapes=[
            vm((chan, rows, LANE), BF),
            vm((3 * LANE, wide), BF),
            vm((9 * pad, height * LANE), BF),
            vm((9 * pad, 3 * LANE), BF),
            vm((3 * channels, 9 * pad), BF),
            vm((3, channels * height, LANE), F32),
            vm((3, pad * height, LANE), F32),
            vm((max(9 * pad, 3 * channels), height * LANE), F32),
            vm((3, pad * height, LANE), F32),
            vm((channels * height, LANE), F32),
            vm((2, rows, LANE), BF),
            vm((2, rows, LANE), BF),
            vm((2, rows, LANE), BF),
            vm((space * chunk, LANE), F32),
            vm((space, chunk, LANE), BF),
            vm((space, chunk, LANE), BF),
            vm((space, chunk, LANE), BF),
            vm((chan, rows, LANE), BF),
            vm((chan, rows, LANE), BF),
            dma((chan,)), dma((chan,)), dma((2,)), dma((2,)), dma((2,)), dma((2,)),
            dma((space,)), dma((space,)), dma((space,)), dma((space,)),
            dma((chan,)), dma((chan,)),
        ],
        compiler_params=pltpu.CompilerParams(
            collective_id=0, has_side_effects=True, vmem_limit_bytes=40 * 2**20),
    )(activation.reshape(rows, width), cotangent.reshape(rows, width),
      weights.reshape(27, channels, channels))
    field = (1, blk, height, width)
    grads = jnp.swapaxes(grads.reshape(3, 3, 3, blk, channels), 3, 4)
    return out.reshape(field), back.reshape(field), grads


def solution(mesh):
    field = P("space", "chan", None, None)
    return jax.shard_map(
        functools.partial(body, mesh.shape["space"], mesh.shape["chan"]),
        mesh=mesh,
        in_specs=(field, P(), field),
        out_specs=(field, field, P(None, None, None, None, "chan")),
        check_vma=False,
    )
```
